128 devices in a mesh: dp: 32 (over y, z, core), expert: 4 (over x).
Axes of the slice: x: 4, y: 4, z: 4, core: 2. Of those that a mesh axis runs over, the one named last changes fastest.
Arguments:
- tokens: bfloat16 [32768, 7168], P(('dp', 'expert')), may hold values from -6 to 6
- routes: int32 [32768, 8], P(('dp', 'expert')), may hold values from 0 to 255, as said below
- slot_ids: int32 [32768, 8], P(('dp', 'expert')), may hold values from -1 to 15, as said below
- gate_weight: bfloat16 [4, 2048, 7168], P('expert', 'dp'), may hold values from -0.0625 to 0.0625
- up_weight: bfloat16 [4, 2048, 7168], P('expert', 'dp'), may hold values from -0.0625 to 0.0625
Outputs:
- input_hessian: float32 [4, 7168, 7168], P('expert', 'dp')
- down_hessian: float32 [4, 2048, 2048], P('expert', 'dp')
The draws below stay inside these ranges and needn't reach their ends.
Inputs may be any that keep to these rules, and one draw needn't show every extreme that they name: `routes`: distinct ids in each row. On each device, no window expert is named by more than 16 tokens, and in every group of 4 consecutive devices along dp+expert (one index of dp) some window expert is named by exactly 16 tokens on every one of them. Every window expert is named on every device. `slot_ids`: for a choice of a window expert: on each device, the tokens naming that expert hold the slots 0 to n - 1, each once; for ids of 4 or more the slot is -1.
All inputs are finite; a program needn't handle non-finite values.
Results may differ from the reference program's by a relative error of at most 0.0038.
Values may be sent and summed in bfloat16 or wider, within the bound.
No kernel may reach another device: no remote copies, remote signals or barrier semaphores. Data moves between devices by JAX's collectives and lax.ppermute only.
A program may use at most 192 MiB of HBM per device.

```python
import jax
import jax.numpy as jnp
from jax import lax

D = 7168
FF = 2048
EXPERTS_ALL = 256
TOP = 8
TOK_DEV = 256
CAP = 16
EXPERTS = 4
TOKENS = 32768


def routing(key):
    blocks = TOKENS // TOK_DEV
    keys = jax.random.split(key, 5)
    index = jnp.arange(blocks, dtype=jnp.int32)
    upper = jnp.maximum(1, CAP // 3 + (CAP - CAP // 3) * index // max(blocks - 1, 1))
    lower = jnp.maximum(1, upper // 2)
    raw = jax.random.randint(keys[0], (blocks, EXPERTS), 0, 1 << 30)
    counts = raw % (upper - lower + 1)[:, None] + lower[:, None]
    full_pick = jax.random.randint(keys[1], (blocks // EXPERTS,), 0, EXPERTS)
    full_each = full_pick[index // EXPERTS]
    counts = jnp.where(jnp.arange(EXPERTS)[None, :] == full_each[:, None], CAP, counts)
    scores = jax.random.randint(keys[2], (blocks, EXPERTS, TOK_DEV), 0, 1 << 20) * TOK_DEV + jnp.arange(TOK_DEV, dtype=jnp.int32)
    ranking = jnp.argsort(jnp.argsort(scores, axis=2, stable=True), axis=2, stable=True).astype(jnp.int32)
    chosen = ranking < counts[:, :, None]
    chosen_t = jnp.transpose(chosen, (0, 2, 1))
    ranking_t = jnp.transpose(ranking, (0, 2, 1))
    others = EXPERTS_ALL - EXPERTS
    other_scores = jax.random.randint(keys[3], (blocks, TOK_DEV, others), 0, 1 << 20) * others + jnp.arange(others, dtype=jnp.int32)
    fill_ids = lax.top_k(other_scores, TOP)[1].astype(jnp.int32) + EXPERTS
    window_ids = jnp.broadcast_to(jnp.arange(EXPERTS, dtype=jnp.int32), (blocks, TOK_DEV, EXPERTS))
    cand_ids = jnp.concatenate([window_ids, fill_ids], axis=2)
    cand_slots = jnp.concatenate([ranking_t, jnp.full((blocks, TOK_DEV, TOP), -1, jnp.int32)], axis=2)
    order_key = jnp.concatenate([jnp.where(chosen_t, 0, 2), jnp.ones((blocks, TOK_DEV, TOP), jnp.int32)], axis=2)
    order = jnp.argsort(order_key, axis=2, stable=True)[:, :, :TOP]
    picked_ids = jnp.take_along_axis(cand_ids, order, axis=2)
    picked_slots = jnp.take_along_axis(cand_slots, order, axis=2)
    shuffle = jax.random.randint(keys[4], (blocks, TOK_DEV, TOP), 0, 1 << 20) * TOP + jnp.arange(TOP, dtype=jnp.int32)
    mixing = jnp.argsort(shuffle, axis=2, stable=True)
    picked_ids = jnp.take_along_axis(picked_ids, mixing, axis=2).reshape(TOKENS, TOP)
    picked_slots = jnp.take_along_axis(picked_slots, mixing, axis=2).reshape(TOKENS, TOP)
    return (picked_ids.astype(jnp.int32), picked_slots.astype(jnp.int32))


def draw_routes(key, part):
    return routing(key)[0]


def draw_slot_ids(key, part):
    return routing(key)[1]


def levels(stream_key, shape, cuts, low, top_value):
    loudness, own = 1.0, jax.random.fold_in(stream_key, 6)
    for dim, blocks in cuts:
        heights = jnp.exp(jax.random.uniform(jax.random.fold_in(own, dim), (blocks,), jnp.float32, low / len(cuts), top_value / len(cuts)))
        loudness = loudness * jnp.repeat(heights, shape[dim] // blocks).reshape([-1 if axis == dim else 1 for axis in range(len(shape))])
    return loudness


def gaussian(own_key, extent, width, bound, pieces=(), held_as=jnp.bfloat16):
    factor_of = levels(own_key, extent, pieces, -0.22, 0.18) if pieces else 1.0
    drawn = jax.random.normal(own_key, extent, jnp.float32) * width * factor_of
    return jnp.minimum(jnp.maximum(drawn, -bound), bound).astype(held_as)


def setup_inputs(seed: int = 0) -> dict:
    key_of = jax.random.split(jax.random.key(seed), 6)
    tokens = gaussian(key_of[0], (TOKENS, D), 1.0, 6.0, ((0, 128),))
    routes = draw_routes(jax.random.fold_in(key_of[5], 71), 0)
    slot_ids = draw_slot_ids(jax.random.fold_in(key_of[5], 71), 0)
    gate_weight = gaussian(key_of[3], (EXPERTS, FF, D), D ** -0.5, 0.0625, ((0, 4), (1, 32)))
    up_weight = gaussian(key_of[4], (EXPERTS, FF, D), D ** -0.5, 0.0625, ((0, 4), (1, 32)))
    return {"tokens": tokens, "routes": routes, "slot_ids": slot_ids, "gate_weight": gate_weight, "up_weight": up_weight}


def reference(tokens, routes, slot_ids, gate_weight, up_weight):
    blocks = TOKENS // TOK_DEV
    owner_block = (jnp.arange(TOKENS, dtype=jnp.int32) // TOK_DEV).astype(jnp.int32)
    hessians = []
    downs = []
    for expert_id in range(EXPERTS):
        chosen = routes == expert_id
        member = jnp.any(chosen, axis=1)
        slot_here = jnp.sum(jnp.where(chosen, slot_ids, 0), axis=1).astype(jnp.int32)
        target = jnp.where(member, owner_block * CAP + slot_here, blocks * CAP).astype(jnp.int32)
        buffer = jnp.zeros((blocks * CAP + 1, D), jnp.bfloat16).at[target].set(tokens)[: blocks * CAP]
        routed = jnp.sum(member.astype(jnp.float32))
        factor = 2.0 / routed
        gram = jnp.dot(buffer.T, buffer, preferred_element_type=jnp.float32)
        hessians.append(gram * factor)
        gate = jnp.dot(buffer, gate_weight[expert_id].T, preferred_element_type=jnp.float32)
        upward = jnp.dot(buffer, up_weight[expert_id].T, preferred_element_type=jnp.float32)
        hidden = (jax.nn.silu(gate) * upward).astype(jnp.bfloat16)
        downs.append(jnp.dot(hidden.T, hidden, preferred_element_type=jnp.float32) * factor)
    return jnp.stack(hessians), jnp.stack(downs)
```

```python
import functools

import jax
import jax.numpy as jnp
from jax import lax
from jax.experimental import pallas as pl
from jax.experimental.pallas import tpu as pltpu
from jax.sharding import PartitionSpec as P

CAP = 16
WIDTH = 7168
FLAG = 128
SENT = WIDTH + FLAG
FF = 2048
SIDE = 4
CHIPS = 16
GRAM_ROWS = 448
WINDOW = 512
F32 = jnp.float32
BF16 = jnp.bfloat16
ORIGIN = (0, -1, 1, 2)
VMEM = pl.BlockSpec(memory_space=pltpu.VMEM)
SMEM = pl.BlockSpec(memory_space=pltpu.SMEM)
PARAMS = pltpu.CompilerParams(vmem_limit_bytes=60 * 1024 * 1024)


def device(y, z, core):
    return ((y % SIDE) * SIDE + z % SIDE) * 2 + core


def steps(first, second):
    return [
        (device(y, z, core), device(y + move[0], z + move[1], core))
        for y in range(SIDE)
        for z in range(SIDE)
        for core, move in enumerate((first, second))
    ]


def major(value, step):
    return lax.ppermute(value, "dp", steps((step, 0), (0, step)))


def minor(value, step):
    return lax.ppermute(value, "dp", steps((0, step), (step, 0)))


def along_y(value, step):
    return lax.ppermute(value, "dp", steps((step, 0), (step, 0)))


def along_z(value, step):
    return lax.ppermute(value, "dp", steps((0, step), (0, step)))


def sibling(value):
    return lax.ppermute(value, "dp", [(i, i ^ 1) for i in range(2 * CHIPS)])


def ring(value, move):
    half = value.shape[0] // 2
    up = move(value, 1)
    down = move(value, -1)
    return (up, down, move(up[:half], 1), move(down[half:], -1))


def dispatch_kernel(where, routes, slots, tokens, *outs):
    wanted = jnp.where(routes[...] < 4, routes[...] * CAP + slots[...], -1)
    lane = lax.broadcasted_iota(jnp.int32, (4 * CAP, 1), 0)
    target = ((lane // CAP + where[0]) % 4) * CAP + lane % CAP
    hit = wanted[0:1, :] == target
    for k in range(1, 8):
        hit = hit | (wanted[k : k + 1, :] == target)
    one_hot = hit.astype(F32).astype(BF16)
    flag = jnp.max(hit.astype(F32), axis=1, keepdims=True)
    flag = jnp.broadcast_to(flag, (4 * CAP, FLAG)).astype(BF16)
    for start in range(0, WIDTH, 1024):
        rows = jnp.dot(
            one_hot, tokens[:, start : start + 1024], preferred_element_type=F32
        ).astype(BF16)
        for j, out in enumerate(outs):
            out[:, start : start + 1024] = rows[j * CAP : (j + 1) * CAP]
    for j, out in enumerate(outs):
        out[:, WIDTH:] = flag[j * CAP : (j + 1) * CAP]


def dispatch(where, routes, slots, tokens):
    return pl.pallas_call(
        dispatch_kernel,
        out_shape=[jax.ShapeDtypeStruct((CAP, SENT), BF16)] * 4,
        in_specs=[SMEM, VMEM, VMEM, VMEM],
        out_specs=[VMEM] * 4,
        compiler_params=PARAMS,
    )(where, routes.T, slots.T, tokens)


def hidden_kernel(where, p0, p1, p2, p3, p4, g, gs, u, us, hidden, window, count):
    pieces = (p0, p1, p2, p3, p4)
    base = pl.multiple_of(where[0], 128)
    total = jnp.zeros((256, 256), F32)
    for start in range(0, WIDTH, 1024):
        rows = jnp.concatenate([p[:, start : start + 1024] for p in pieces], 0)
        weights = jnp.concatenate([w[:, start : start + 1024] for w in (g, gs, u, us)], 0)
        total += lax.dot_general(
            rows, weights, (((1,), (1,)), ((), ())), preferred_element_type=F32
        )
    gate, upward = total[:, :128], total[:, 128:]
    value = gate / (1.0 + jnp.exp(-gate)) * upward
    value = jnp.where(where[1] == 1, pltpu.roll(value, 64, 1), value)
    hidden[...] = value.astype(BF16)
    window[...] = jnp.concatenate([p[:, pl.ds(base, WINDOW)] for p in pieces], 0)
    flags = jnp.concatenate([p[:, WIDTH:] for p in pieces], 0).astype(F32)
    count[...] = jnp.broadcast_to(jnp.sum(flags, axis=0, keepdims=True), (8, FLAG))


def hidden_work(where, pieces, weights):
    return pl.pallas_call(
        hidden_kernel,
        out_shape=[
            jax.ShapeDtypeStruct((256, 128), BF16),
            jax.ShapeDtypeStruct((256, WINDOW), BF16),
            jax.ShapeDtypeStruct((8, FLAG), F32),
        ],
        in_specs=[SMEM] + [VMEM] * 9,
        out_specs=[VMEM] * 3,
        compiler_params=PARAMS,
        cost_estimate=pl.CostEstimate(
            flops=2 * 256 * 256 * WIDTH, bytes_accessed=8 << 20, transcendentals=256 * 128
        ),
    )(where, *pieces, *weights)


def order_kernel(offsets, h0, h1, h2, h3, out):
    for i, h in enumerate((h0, h1, h2, h3)):
        for j in range(4):
            start = pl.multiple_of(offsets[4 * i + j], 64)
            out[pl.ds(start, 64), :] = h[64 * j : 64 * j + 64, :]


def order(offsets, parts):
    return pl.pallas_call(
        order_kernel,
        out_shape=jax.ShapeDtypeStruct((1024, 128), BF16),
        in_specs=[SMEM] + [VMEM] * 4,
        out_specs=VMEM,
        compiler_params=PARAMS,
    )(offsets, *parts)


def down_kernel(where, own, z0, z1, z2, z3, y0, y1, y2, y3, n0, n1, n2, n3, keep, send, tile):
    core = where[1]
    left = jnp.concatenate(
        [own[...], z0[...], z1[...], jnp.concatenate([z2[...], z3[...]], 0)], 1
    )
    right = jnp.concatenate(
        [own[...], y0[...], y1[...], jnp.concatenate([y2[...], y3[...]], 0)], 1
    )
    tile[...] = lax.dot_general(
        left, right, (((0,), (0,)), ((), ())), preferred_element_type=F32
    )
    for j in range(4):
        keep[64 * j : 64 * j + 64, :] = tile[pl.ds(pl.multiple_of(128 * j + 64 * core, 64), 64), :]
        send[64 * j : 64 * j + 64, :] = tile[
            pl.ds(pl.multiple_of(128 * j + 64 - 64 * core, 64), 64), :
        ]
    count = n0[...] + n1[...] + n2[...] + n3[...]
    count = jnp.concatenate([count] * 4, 1)
    keep[256:, :] = count
    send[256:, :] = count


def down_work(where, own, ring_z, ring_y, counts):
    return pl.pallas_call(
        down_kernel,
        out_shape=[jax.ShapeDtypeStruct((264, 512), F32)] * 2,
        in_specs=[SMEM] + [VMEM] * 13,
        out_specs=[VMEM] * 2,
        scratch_shapes=[pltpu.VMEM((512, 512), F32)],
        compiler_params=PARAMS,
        cost_estimate=pl.CostEstimate(
            flops=2 * 512 * 512 * 1024, bytes_accessed=4 << 20, transcendentals=0
        ),
    )(where, own, *ring_z, *ring_y, *counts)


def place_kernel(offsets, b0, b1, b2, b3, factor, out):
    for j, block in enumerate((b0, b1, b2, b3)):
        for i in range(4):
            start = pl.multiple_of(offsets[4 * j + i], 128)
            out[0, :, pl.ds(start, 128)] = block[:, 128 * i : 128 * i + 128] * factor[0, 0]


def place(offsets, blocks, factor):
    return pl.pallas_call(
        place_kernel,
        out_shape=jax.ShapeDtypeStruct((1, 64, FF), F32),
        in_specs=[SMEM] + [VMEM] * 4 + [SMEM],
        out_specs=VMEM,
        compiler_params=PARAMS,
    )(offsets, *blocks, factor)


def gram_kernel(first, count, where, w0, w1, w2, w3, *refs):
    pieces, (keep, send, left, tile) = refs[:20], refs[20:]
    core, shift = where[1], where[2]
    mine = pl.multiple_of(shift + core * 224, 32)
    other = pl.multiple_of(shift + 224 - core * 224, 32)
    for i, w in enumerate((w0, w1, w2, w3)):
        left[:, 256 * i : 256 * i + 256] = w[...].T

    @pl.loop(0, count // 512)
    def _(step):
        start = pl.multiple_of(step * 512, 512)
        here = pl.multiple_of(first + step * 512, 512)
        right = jnp.concatenate([p[:, pl.ds(here, 512)] for p in pieces], 0)
        tile[...] = jnp.dot(left[...], right, preferred_element_type=F32)
        keep[:, pl.ds(start, 512)] = tile[pl.ds(mine, 224), :]
        send[:, pl.ds(start, 512)] = tile[pl.ds(other, 224), :]


def gram_work(where, windows, pieces, first, count):
    return pl.pallas_call(
        functools.partial(gram_kernel, first, count),
        out_shape=[jax.ShapeDtypeStruct((224, count), F32)] * 2,
        in_specs=[SMEM] + [VMEM] * 24,
        out_specs=[VMEM] * 2,
        scratch_shapes=[pltpu.VMEM((WINDOW, 1024), BF16), pltpu.VMEM((WINDOW, 512), F32)],
        compiler_params=PARAMS,
        cost_estimate=pl.CostEstimate(
            flops=2 * 512 * count * 1024, bytes_accessed=8 << 20, transcendentals=0
        ),
    )(where, *windows, *pieces)


def local(tokens, routes, slot_ids, gate_weight, up_weight):
    place_dp = lax.axis_index("dp").astype(jnp.int32)
    place_x = lax.axis_index("expert").astype(jnp.int32)
    core = place_dp % 2
    chip = place_dp // 2
    z, y = chip % SIDE, chip // SIDE
    shift = (chip % 2) * 64
    where = jnp.stack([chip * GRAM_ROWS - shift, core, shift])
    minor_of = jnp.array(ORIGIN * 4, jnp.int32)
    major_of = jnp.repeat(jnp.array(ORIGIN, jnp.int32), 4)
    from_y = (y + jnp.where(core == 0, major_of, minor_of)) % SIDE
    from_z = (z + jnp.where(core == 0, minor_of, major_of)) % SIDE
    slots_at = (from_y * SIDE + from_z) * 64
    columns_at = (((y + minor_of) % SIDE) * SIDE + (z + major_of) % SIDE) * 128

    gate_own, up_own = gate_weight[0], up_weight[0]
    weights = (gate_own, sibling(gate_own), up_own, sibling(up_own))

    blocks = dispatch(place_x.reshape(1), routes, slot_ids, tokens)
    parts = [blocks[0]]
    for step in (1, 2, 3):
        parts.append(lax.ppermute(blocks[step], "expert", [(i, (i + step) % 4) for i in range(4)]))
    shard = jnp.concatenate(parts, 0)

    up, down, up2, down2 = ring(shard, major)
    groups = []
    for piece in (shard, up, down, jnp.concatenate([up2, down2], 0)):
        groups.append((piece,) + ring(piece, minor))

    hiddens, windows, counts = [], [], []
    for group in groups:
        h, w, n = hidden_work(where, group, weights)
        hiddens.append(h)
        windows.append(w)
        counts.append(n)

    hidden = order(slots_at, hiddens)
    ring_z = ring(hidden, along_z)
    ring_y = ring(hidden, along_y)
    pieces = [piece for group in groups for piece in group]
    halves = []
    for first in (0, WIDTH // 2):
        keep, send = gram_work(where, windows, pieces, first, WIDTH // 2)
        halves.append((keep, sibling(send)))

    down_keep, down_send = down_work(where, hidden, ring_z, ring_y, counts)
    summed = down_keep + sibling(down_send)
    factor = (2.0 / summed[256, 0]).reshape(1, 1)
    down_blocks = [
        summed[:64],
        along_z(summed[128:192], 1),
        along_z(summed[64:128], -1),
        along_z(summed[192:256], 2),
    ]
    down_rows = place(columns_at, down_blocks, factor)
    gram = jnp.concatenate([(keep + got) * factor for keep, got in halves], 1)
    return gram[None], down_rows


def solution(mesh):
    in_specs = (
        P(("dp", "expert"), None),
        P(("dp", "expert"), None),
        P(("dp", "expert"), None),
        P("expert", "dp", None),
        P("expert", "dp", None),
    )
    out_specs = (P("expert", "dp", None), P("expert", "dp", None))
    return jax.shard_map(local, mesh=mesh, in_specs=in_specs, out_specs=out_specs, check_vma=False)
```

```python
import functools

import jax
import jax.numpy as jnp
from jax import lax
from jax.experimental import pallas as pl
from jax.experimental.pallas import tpu as pltpu
from jax.sharding import PartitionSpec as P

CAP = 16
WIDTH = 7168
FLAG = 128
SENT = WIDTH + FLAG
FF = 2048
SIDE = 4
CHIPS = 16
GRAM_ROWS = 448
WINDOW = 512
F32 = jnp.float32
BF16 = jnp.bfloat16
ORIGIN = (0, -1, 1, 2)
VMEM = pl.BlockSpec(memory_space=pltpu.VMEM)
SMEM = pl.BlockSpec(memory_space=pltpu.SMEM)
CHUNK = 1024


def params(mib):
    return pltpu.CompilerParams(vmem_limit_bytes=mib * 1024 * 1024)


def spot():
    here = lax.axis_index("dp")
    return here // 8, (here // 2) % SIDE, here % 2


def gram_start():
    y, z, _ = spot()
    chip = y * SIDE + z
    shift = (chip % 2) * 64
    return chip * GRAM_ROWS - shift, shift


def pinned(values):
    return [pltpu.with_memory_space_constraint(v, pltpu.VMEM) for v in values]


def device(y, z, core):
    return ((y % SIDE) * SIDE + z % SIDE) * 2 + core


def steps(first, second):
    return [
        (device(y, z, core), device(y + move[0], z + move[1], core))
        for y in range(SIDE)
        for z in range(SIDE)
        for core, move in enumerate((first, second))
    ]


def major(value, step):
    return lax.ppermute(value, "dp", steps((step, 0), (0, step)))


def minor(value, step):
    return lax.ppermute(value, "dp", steps((0, step), (step, 0)))


def along_y(value, step):
    return lax.ppermute(value, "dp", steps((step, 0), (step, 0)))


def along_z(value, step):
    return lax.ppermute(value, "dp", steps((0, step), (0, step)))


def sibling(value):
    return lax.ppermute(value, "dp", [(i, i ^ 1) for i in range(2 * CHIPS)])


def ring(value, move):
    half = value.shape[0] // 2
    up = move(value, 1)
    down = move(value, -1)
    return (up, down, move(up[:half], 1), move(down[half:], -1))


def direct_ring(value, move):
    return move(value, 1), move(value, -1), move(value, 2)


def dispatch_kernel(routes, slots, tokens, *outs):
    wanted = jnp.where(routes[...] < 4, routes[...] * CAP + slots[...], -1)
    lane = lax.broadcasted_iota(jnp.int32, (4 * CAP, 1), 0)
    target = ((lane // CAP + lax.axis_index("expert")) % 4) * CAP + lane % CAP
    hit = wanted[0:1, :] == target
    for k in range(1, 8):
        hit = hit | (wanted[k : k + 1, :] == target)
    one_hot = hit.astype(F32).astype(BF16)
    flag = jnp.max(hit.astype(F32), axis=1, keepdims=True)
    flag = jnp.broadcast_to(flag, (4 * CAP, FLAG)).astype(BF16)
    for start in range(0, WIDTH, 1024):
        rows = jnp.dot(
            one_hot, tokens[:, start : start + 1024], preferred_element_type=F32
        ).astype(BF16)
        for j, out in enumerate(outs):
            out[:, start : start + 1024] = rows[j * CAP : (j + 1) * CAP]
    for j, out in enumerate(outs):
        out[:, WIDTH:] = flag[j * CAP : (j + 1) * CAP]


def dispatch(routes, slots, tokens):
    return pl.pallas_call(
        dispatch_kernel,
        out_shape=[jax.ShapeDtypeStruct((CAP, SENT), BF16)] * 4,
        in_specs=[VMEM] * 3,
        out_specs=[VMEM] * 4,
        compiler_params=params(32),
    )(routes.T, slots.T, tokens)


def hidden_kernel(group, *refs):
    size = len(refs) - (8 if group else 7)
    pieces, (g, gs, u, us) = refs[:size], refs[size : size + 4]
    hidden, window, count = refs[-3:]
    y, z, core = spot()
    base, _ = gram_start()
    total = jnp.zeros((256, 256), F32)
    for start in range(0, WIDTH, CHUNK):
        rows = jnp.concatenate([p[:, start : start + CHUNK] for p in pieces], 0)
        weights = jnp.concatenate([w[:, start : start + CHUNK] for w in (g, gs, u, us)], 0)
        total += lax.dot_general(
            rows, weights, (((1,), (1,)), ((), ())), preferred_element_type=F32
        )
    gate, upward = total[:, :128], total[:, 128:]
    value = gate / (1.0 + jnp.exp(-gate)) * upward
    value = jnp.where(core == 1, pltpu.roll(value, 64, 1), value).astype(BF16)
    seen = jnp.concatenate([p[:, WIDTH:] for p in pieces], 0).astype(F32)
    count[...] = jnp.broadcast_to(jnp.sum(seen, axis=0, keepdims=True), (16, FLAG))
    if group:
        hidden[...] = refs[size + 4][...]
    for j in range(4):
        far = (jnp.where(core == 0, y, z) + ORIGIN[group] + SIDE) % SIDE
        near = (jnp.where(core == 0, z, y) + ORIGIN[j] + SIDE) % SIDE
        slot = jnp.where(core == 0, far * SIDE + near, near * SIDE + far)
        hidden[pl.ds(pl.multiple_of(slot * 64, 64), 64), :] = value[64 * j : 64 * j + 64]
    base = pl.multiple_of(base, 128)
    window[...] = jnp.concatenate([p[:, pl.ds(base, WINDOW)] for p in pieces], 0).T


def hidden_work(group, pieces, weights, before):
    return pl.pallas_call(
        functools.partial(hidden_kernel, group),
        out_shape=[
            jax.ShapeDtypeStruct((1024, 128), BF16),
            jax.ShapeDtypeStruct((WINDOW, 256), BF16),
            jax.ShapeDtypeStruct((16, FLAG), F32),
        ],
        in_specs=[VMEM] * (len(pieces) + 4 + len(before)),
        out_specs=[VMEM] * 3,
        compiler_params=params(12),
        cost_estimate=pl.CostEstimate(
            flops=2 * 256 * 256 * WIDTH, bytes_accessed=8 << 20, transcendentals=256 * 128
        ),
    )(*pinned(pieces), *pinned(weights), *pinned(before))


def down_kernel(own, z0, z1, z2, y0, y1, y2, n0, n1, n2, n3, keep, send, tile):
    core = spot()[2]
    left = jnp.concatenate([own[...], z0[...], z1[...], z2[...]], 1)
    right = jnp.concatenate([own[...], y0[...], y1[...], y2[...]], 1)
    tile[...] = lax.dot_general(
        left, right, (((0,), (0,)), ((), ())), preferred_element_type=F32
    )
    for j in range(4):
        mine = pl.multiple_of(128 * j + 64 * core, 64)
        other = pl.multiple_of(128 * j + 64 - 64 * core, 64)
        keep[64 * j : 64 * j + 64, :] = tile[pl.ds(mine, 64), :]
        send[64 * j : 64 * j + 64, :] = tile[pl.ds(other, 64), :].astype(BF16)
    counts = jnp.concatenate([n0[...], n1[...], n2[...], n3[...]], 1)
    keep[256:, :] = counts
    send[256:, :] = counts.astype(BF16)


def down_work(own, ring_z, ring_y, counts):
    return pl.pallas_call(
        down_kernel,
        out_shape=[
            jax.ShapeDtypeStruct((272, 512), F32),
            jax.ShapeDtypeStruct((272, 512), BF16),
        ],
        in_specs=[VMEM] * 11,
        out_specs=[VMEM] * 2,
        scratch_shapes=[pltpu.VMEM((512, 512), F32)],
        compiler_params=params(12),
        cost_estimate=pl.CostEstimate(
            flops=2 * 512 * 512 * 1024, bytes_accessed=4 << 20, transcendentals=0
        ),
    )(*pinned((own, *ring_z, *ring_y, *counts)))


def sum_kernel(keep, got, *outs):
    for j in range(4):
        rows = pl.ds(64 * j, 64)
        outs[j][...] = (keep[rows, :] + got[rows, :].astype(F32)).astype(outs[j].dtype)
    counts = keep[256:264, :] + got[256:, :].astype(F32)[:8]
    total = sum(counts[:, 128 * i : 128 * i + 128] for i in range(4))
    outs[4][...] = 2.0 / total


def sum_blocks(keep, got):
    return pl.pallas_call(
        sum_kernel,
        out_shape=[jax.ShapeDtypeStruct((64, 512), F32 if j == 0 else BF16) for j in range(4)]
        + [jax.ShapeDtypeStruct((8, 128), F32)],
        in_specs=[VMEM] * 2,
        out_specs=[VMEM] * 5,
        compiler_params=params(8),
    )(*pinned((keep, got)))


def place_kernel(b0, b1, b2, b3, factor, out):
    y, z, _ = spot()
    for j, block in enumerate((b0, b1, b2, b3)):
        for i in range(4):
            from_y = (y + ORIGIN[i] + SIDE) % SIDE
            from_z = (z + ORIGIN[j] + SIDE) % SIDE
            start = pl.multiple_of((from_y * SIDE + from_z) * 128, 128)
            part = block[:, 128 * i : 128 * i + 128].astype(F32)
            out[0, :, pl.ds(start, 128)] = part * factor[0:1, :]


def place(blocks, factor):
    return pl.pallas_call(
        place_kernel,
        out_shape=jax.ShapeDtypeStruct((1, 64, FF), F32),
        in_specs=[VMEM] * 5,
        out_specs=VMEM,
        compiler_params=params(8),
    )(*pinned((*blocks, factor)))


def gram_kernel(mine, *refs):
    size = len(refs) - (3 if mine else 1)
    windows, pieces, rest = refs[:4], refs[4:size], refs[size:]
    core = spot()[2]
    _, shift = gram_start()
    first = shift + core * 224 if mine else shift + 224 - core * 224
    first = pl.multiple_of(first, 32)
    left = jnp.concatenate([w[pl.ds(first, 224), :] for w in windows], 1)
    here = pl.ds(pl.multiple_of(pl.program_id(0) * CHUNK, CHUNK), CHUNK)
    right = jnp.concatenate([p[:, here] for p in pieces], 0)
    part = jnp.dot(left, right, preferred_element_type=F32)
    if mine:
        got, factor, out = rest
        out[0, :, :] = (part + got[:, here].astype(F32)) * factor[0:1, 0:1]
    else:
        rest[0][...] = part.astype(BF16)


def gram_work(windows, pieces, got=None, factor=None):
    mine = got is not None
    shape = (224, WIDTH)
    if mine:
        out_spec = pl.BlockSpec((1, 224, CHUNK), lambda n: (0, 0, n))
    else:
        out_spec = pl.BlockSpec((224, CHUNK), lambda n: (0, n))
    return pl.pallas_call(
        functools.partial(gram_kernel, mine),
        grid=(WIDTH // CHUNK,),
        out_shape=jax.ShapeDtypeStruct((1,) + shape, F32) if mine else jax.ShapeDtypeStruct(shape, BF16),
        in_specs=[VMEM] * (4 + len(pieces)) + ([VMEM] * 2 if mine else []),
        out_specs=out_spec,
        compiler_params=params(10),
        cost_estimate=pl.CostEstimate(
            flops=2 * 224 * WIDTH * 1024, bytes_accessed=24 << 20, transcendentals=0
        ),
    )(*pinned(windows), *pinned(pieces), *(pinned((got, factor)) if mine else ()))


def after(value, done):
    return lax.optimization_barrier((value, done))


def local(tokens, routes, slot_ids, gate_weight, up_weight):
    gate_own, up_own = gate_weight[0], up_weight[0]
    weights = (gate_own, sibling(gate_own), up_own, sibling(up_own))

    blocks = dispatch(routes, slot_ids, tokens)
    parts = [blocks[0]]
    for step in (1, 2, 3):
        parts.append(lax.ppermute(blocks[step], "expert", [(i, (i + step) % 4) for i in range(4)]))
    shard = jnp.concatenate(parts, 0)

    up, down, up2, down2 = ring(shard, major)
    groups = []
    for piece in (shard, up, down, jnp.concatenate([up2, down2], 0)):
        groups.append((piece,) + ring(piece, minor))
    windows, counts, before = [], [], ()
    for index, group in enumerate(groups):
        hidden, window, count = hidden_work(index, group, weights, before)
        before = (hidden,)
        windows.append(window)
        counts.append(count)

    ring_z = direct_ring(hidden, along_z)
    ring_y = direct_ring(hidden, along_y)
    pieces = [piece for group in groups for piece in group]
    send, _ = after(gram_work(windows, pieces), (ring_z[:2], ring_y[:2]))
    got = sibling(send)

    down_keep, down_send = down_work(hidden, ring_z, ring_y, counts)
    *sums, factor = sum_blocks(down_keep, sibling(down_send))
    down_blocks = [
        sums[0],
        along_z(sums[2], 1),
        along_z(sums[1], -1),
        along_z(sums[3], 2),
    ]
    gram = gram_work(windows, pieces, got, factor)
    factor, gram = after(factor, gram)
    return gram, place(down_blocks, factor)


def solution(mesh):
    in_specs = (
        P(("dp", "expert"), None),
        P(("dp", "expert"), None),
        P(("dp", "expert"), None),
        P("expert", "dp", None),
        P("expert", "dp", None),
    )
    out_specs = (P("expert", "dp", None), P("expert", "dp", None))
    return jax.shard_map(local, mesh=mesh, in_specs=in_specs, out_specs=out_specs, check_vma=False)
```

```python
import functools

import jax
import jax.numpy as jnp
from jax import lax
from jax.experimental import pallas as pl
from jax.experimental.pallas import tpu as pltpu
from jax.sharding import PartitionSpec as P

CAP = 16
WIDTH = 7168
FLAG = 128
SENT = WIDTH + FLAG
FF = 2048
SIDE = 4
CHIPS = 16
GRAM_ROWS = 448
WINDOW = 512
F32 = jnp.float32
BF16 = jnp.bfloat16
ORIGIN = (0, -1, 1, 2)
VMEM = pl.BlockSpec(memory_space=pltpu.VMEM)
SMEM = pl.BlockSpec(memory_space=pltpu.SMEM)
CHUNK = 1024


def params(mib):
    return pltpu.CompilerParams(vmem_limit_bytes=mib * 1024 * 1024)


def spot():
    here = lax.axis_index("dp")
    return here // 8, (here // 2) % SIDE, here % 2


def gram_start():
    y, z, _ = spot()
    chip = y * SIDE + z
    shift = (chip % 2) * 64
    return chip * GRAM_ROWS - shift, shift


def pinned(values):
    return [pltpu.with_memory_space_constraint(v, pltpu.VMEM) for v in values]


def device(y, z, core):
    return ((y % SIDE) * SIDE + z % SIDE) * 2 + core


def steps(first, second):
    return [
        (device(y, z, core), device(y + move[0], z + move[1], core))
        for y in range(SIDE)
        for z in range(SIDE)
        for core, move in enumerate((first, second))
    ]


def major(value, step):
    return lax.ppermute(value, "dp", steps((step, 0), (0, step)))


def minor(value, step):
    return lax.ppermute(value, "dp", steps((0, step), (step, 0)))


def along_y(value, step):
    return lax.ppermute(value, "dp", steps((step, 0), (step, 0)))


def along_z(value, step):
    return lax.ppermute(value, "dp", steps((0, step), (0, step)))


def sibling(value):
    return lax.ppermute(value, "dp", [(i, i ^ 1) for i in range(2 * CHIPS)])


def ring(value, move):
    half = value.shape[0] // 2
    up = move(value, 1)
    down = move(value, -1)
    return (up, down, move(up[:half], 1), move(down[half:], -1))


def dispatch_kernel(routes, slots, tokens, *outs):
    wanted = jnp.where(routes[...] < 4, routes[...] * CAP + slots[...], -1)
    lane = lax.broadcasted_iota(jnp.int32, (4 * CAP, 1), 0)
    target = ((lane // CAP + lax.axis_index("expert")) % 4) * CAP + lane % CAP
    hit = wanted[0:1, :] == target
    for k in range(1, 8):
        hit = hit | (wanted[k : k + 1, :] == target)
    one_hot = hit.astype(F32).astype(BF16)
    flag = jnp.max(hit.astype(F32), axis=1, keepdims=True)
    flag = jnp.broadcast_to(flag, (4 * CAP, FLAG)).astype(BF16)
    for start in range(0, WIDTH, 1024):
        rows = jnp.dot(
            one_hot, tokens[:, start : start + 1024], preferred_element_type=F32
        ).astype(BF16)
        for j, out in enumerate(outs):
            out[:, start : start + 1024] = rows[j * CAP : (j + 1) * CAP]
    for j, out in enumerate(outs):
        out[:, WIDTH:] = flag[j * CAP : (j + 1) * CAP]


def dispatch(routes, slots, tokens):
    in_hbm = [pltpu.with_memory_space_constraint(v.T, pltpu.HBM) for v in (routes, slots)]
    return pl.pallas_call(
        dispatch_kernel,
        out_shape=[jax.ShapeDtypeStruct((CAP, SENT), BF16)] * 4,
        in_specs=[VMEM] * 3,
        out_specs=[VMEM] * 4,
        compiler_params=params(32),
    )(*in_hbm, *pinned([tokens]))


def hidden_kernel(spots, first, *refs):
    size = len(refs) - (7 if first else 8)
    height = 64 * len(spots)
    pieces, (g, gs, u, us) = refs[:size], refs[size : size + 4]
    hidden, window, count = refs[-3:]
    y, z, core = spot()
    base, _ = gram_start()
    total = jnp.zeros((height, 256), F32)
    for start in range(0, WIDTH, CHUNK):
        rows = jnp.concatenate([p[:, start : start + CHUNK] for p in pieces], 0)
        weights = jnp.concatenate([w[:, start : start + CHUNK] for w in (g, gs, u, us)], 0)
        total += lax.dot_general(
            rows, weights, (((1,), (1,)), ((), ())), preferred_element_type=F32
        )
    gate, upward = total[:, :128], total[:, 128:]
    value = gate / (1.0 + jnp.exp(-gate)) * upward
    value = jnp.where(core == 1, pltpu.roll(value, 64, 1), value).astype(BF16)
    seen = jnp.concatenate([p[:, WIDTH:] for p in pieces], 0).astype(F32)
    for part in range(height // 256):
        total_seen = jnp.sum(seen[256 * part : 256 * part + 256], axis=0, keepdims=True)
        count[:, FLAG * part : FLAG * part + FLAG] = jnp.broadcast_to(total_seen, (16, FLAG))
    if not first:
        hidden[...] = refs[size + 4][...]
    for j, (far, near) in enumerate(spots):
        far = (jnp.where(core == 0, y, z) + far + SIDE) % SIDE
        near = (jnp.where(core == 0, z, y) + near + SIDE) % SIDE
        slot = jnp.where(core == 0, far * SIDE + near, near * SIDE + far)
        hidden[pl.ds(pl.multiple_of(slot * 64, 64), 64), :] = value[64 * j : 64 * j + 64]
    base = pl.multiple_of(base, 128)
    window[...] = jnp.concatenate([p[:, pl.ds(base, WINDOW)] for p in pieces], 0).T


def hidden_work(spots, pieces, weights, before):
    height = 64 * len(spots)
    return pl.pallas_call(
        functools.partial(hidden_kernel, spots, not before),
        out_shape=[
            jax.ShapeDtypeStruct((1024, 128), BF16),
            jax.ShapeDtypeStruct((WINDOW, height), BF16),
            jax.ShapeDtypeStruct((16, height // 256 * FLAG), F32),
        ],
        in_specs=[VMEM] * (len(pieces) + 4 + len(before)),
        out_specs=[VMEM] * 3,
        compiler_params=params(12),
        cost_estimate=pl.CostEstimate(
            flops=2 * height * 256 * WIDTH,
            bytes_accessed=8 << 20,
            transcendentals=height * 128,
        ),
    )(*pinned(pieces), *pinned(weights), *pinned(before))


def down_kernel(own, z0, z1, z2, y0, y1, y2, *refs):
    counts, (keep, send, tile) = refs[:-3], refs[-3:]
    core = spot()[2]
    left = jnp.concatenate([own[...], z0[...], z1[...], z2[...]], 1)
    right = jnp.concatenate([own[...], y0[...], y1[...], y2[...]], 1)
    tile[...] = lax.dot_general(
        left, right, (((0,), (0,)), ((), ())), preferred_element_type=F32
    )
    for j in range(4):
        mine = pl.multiple_of(128 * j + 64 * core, 64)
        other = pl.multiple_of(128 * j + 64 - 64 * core, 64)
        keep[64 * j : 64 * j + 64, :] = tile[pl.ds(mine, 64), :]
        send[64 * j : 64 * j + 64, :] = tile[pl.ds(other, 64), :].astype(BF16)
    counts = jnp.concatenate([n[...] for n in counts], 1)
    keep[256:, :] = counts
    send[256:, :] = counts.astype(BF16)


def down_work(own, ring_z, ring_y, counts):
    return pl.pallas_call(
        down_kernel,
        out_shape=[
            jax.ShapeDtypeStruct((272, 512), F32),
            jax.ShapeDtypeStruct((272, 512), BF16),
        ],
        in_specs=[VMEM] * (7 + len(counts)),
        out_specs=[VMEM] * 2,
        scratch_shapes=[pltpu.VMEM((512, 512), F32)],
        compiler_params=params(12),
        cost_estimate=pl.CostEstimate(
            flops=2 * 512 * 512 * 1024, bytes_accessed=4 << 20, transcendentals=0
        ),
    )(*pinned((own, *ring_z, *ring_y, *counts)))


def sum_kernel(keep, got, *outs):
    for j in range(4):
        rows = pl.ds(64 * j, 64)
        outs[j][...] = keep[rows, :] + got[rows, :].astype(F32)
    counts = keep[256:264, :] + got[256:, :].astype(F32)[:8]
    total = sum(counts[:, 128 * i : 128 * i + 128] for i in range(4))
    outs[4][...] = 2.0 / total


def sum_blocks(keep, got):
    return pl.pallas_call(
        sum_kernel,
        out_shape=[jax.ShapeDtypeStruct((64, 512), F32)] * 4
        + [jax.ShapeDtypeStruct((8, 128), F32)],
        in_specs=[VMEM] * 2,
        out_specs=[VMEM] * 5,
        compiler_params=params(8),
    )(*pinned((keep, got)))


def place_kernel(b0, b1, b2, b3, factor, out):
    y, z, _ = spot()
    for j, block in enumerate((b0, b1, b2, b3)):
        for i in range(4):
            from_y = (y + ORIGIN[i] + SIDE) % SIDE
            from_z = (z + ORIGIN[j] + SIDE) % SIDE
            start = pl.multiple_of((from_y * SIDE + from_z) * 128, 128)
            part = block[:, 128 * i : 128 * i + 128]
            out[0, :, pl.ds(start, 128)] = part * factor[0:1, :]


def place(blocks, factor):
    return pl.pallas_call(
        place_kernel,
        out_shape=jax.ShapeDtypeStruct((1, 64, FF), F32),
        in_specs=[VMEM] * 5,
        out_specs=VMEM,
        compiler_params=params(8),
    )(*pinned((*blocks, factor)))


def gram_kernel(mine, groups, *refs):
    size = len(refs) - (3 if mine else 1)
    windows, pieces, rest = refs[:groups], refs[groups:size], refs[size:]
    core = spot()[2]
    _, shift = gram_start()
    first = shift + core * 224 if mine else shift + 224 - core * 224
    first = pl.multiple_of(first, 32)
    left = jnp.concatenate([w[pl.ds(first, 224), :] for w in windows], 1)
    here = pl.ds(pl.multiple_of(pl.program_id(0) * CHUNK, CHUNK), CHUNK)
    right = jnp.concatenate([p[:, here] for p in pieces], 0)
    part = jnp.dot(left, right, preferred_element_type=F32)
    if mine:
        got, factor, out = rest
        out[0, :, :] = (part + got[:, here].astype(F32)) * factor[0:1, 0:1]
    else:
        rest[0][...] = part.astype(BF16)


def gram_work(windows, pieces, got=None, factor=None):
    mine = got is not None
    if mine:
        out_shape = jax.ShapeDtypeStruct((1, 224, WIDTH), F32)
        out_spec = pl.BlockSpec((1, 224, CHUNK), lambda n: (0, 0, n))
    else:
        out_shape = jax.ShapeDtypeStruct((224, WIDTH), BF16)
        out_spec = pl.BlockSpec((224, CHUNK), lambda n: (0, n))
    operands = (*windows, *pieces) + ((got, factor) if mine else ())
    return pl.pallas_call(
        functools.partial(gram_kernel, mine, len(windows)),
        grid=(WIDTH // CHUNK,),
        out_shape=out_shape,
        in_specs=[VMEM] * len(operands),
        out_specs=out_spec,
        compiler_params=params(10),
        cost_estimate=pl.CostEstimate(
            flops=2 * 224 * WIDTH * 1024, bytes_accessed=24 << 20, transcendentals=0
        ),
    )(*pinned(operands))


def after(value, done):
    return lax.optimization_barrier((value, done))


def local(tokens, routes, slot_ids, gate_weight, up_weight):
    gate_own, up_own = gate_weight[0], up_weight[0]
    weights = (gate_own, sibling(gate_own), up_own, sibling(up_own))

    blocks = dispatch(routes, slot_ids, tokens)
    parts = [blocks[0]]
    for step in (1, 2, 3):
        parts.append(lax.ppermute(blocks[step], "expert", [(i, (i + step) % 4) for i in range(4)]))
    shard = jnp.concatenate(parts, 0)

    up, down, up2, down2 = ring(shard, major)
    far = jnp.concatenate([up2, down2], 0)
    groups = []
    for origin, piece in zip(ORIGIN, (shard, up, down, far)):
        groups.append(((origin,), (piece,) + ring(piece, minor)))
    windows, counts, before = [], [], ()
    for origins, pieces in groups:
        spots = [(far, near) for near in ORIGIN for far in origins]
        hidden, window, count = hidden_work(spots, pieces, weights, before)
        before = (hidden,)
        windows.append(window)
        counts.append(count)

    z_down, y_down = along_z(hidden, -1), along_y(hidden, -1)
    y_up, z_far, y_far = along_y(hidden, 1), along_z(hidden, 2), along_y(hidden, 2)
    z_up = along_z(hidden, 1)
    hops = (z_up, z_down, z_far, y_up, y_down, y_far)
    pieces = [piece for _, group in groups for piece in group]
    send = gram_work(windows, pieces)
    hops, send = after(hops, send)
    down_keep, down_send = down_work(hidden, hops[:3], hops[3:], counts)
    down_got = sibling(down_send)
    send, down_got = after(send, down_got)
    got = sibling(send)
    *sums, factor = sum_blocks(down_keep, down_got)
    down_blocks = [
        sums[0],
        along_z(sums[2], 1),
        along_z(sums[1], -1),
        along_z(sums[3], 2),
    ]
    gram = gram_work(windows, pieces, got, factor)
    factor, gram = after(factor, gram)
    return gram, place(down_blocks, factor)


def solution(mesh):
    in_specs = (
        P(("dp", "expert"), None),
        P(("dp", "expert"), None),
        P(("dp", "expert"), None),
        P("expert", "dp", None),
        P("expert", "dp", None),
    )
    out_specs = (P("expert", "dp", None), P("expert", "dp", None))
    return jax.shard_map(local, mesh=mesh, in_specs=in_specs, out_specs=out_specs, check_vma=False)
```

```python
import functools

import jax
import jax.numpy as jnp
from jax import lax
from jax.experimental import pallas as pl
from jax.experimental.pallas import tpu as pltpu
from jax.sharding import PartitionSpec as P

CAP = 16
WIDTH = 7168
FLAG = 128
SENT = WIDTH + FLAG
FF = 2048
SIDE = 4
CHIPS = 16
GRAM_ROWS = 448
WINDOW = 512
F32 = jnp.float32
BF16 = jnp.bfloat16
ORIGIN = (0, -1, 1, 2)
VMEM = pl.BlockSpec(memory_space=pltpu.VMEM)
SMEM = pl.BlockSpec(memory_space=pltpu.SMEM)
CHUNK = 1024


def params(mib):
    return pltpu.CompilerParams(vmem_limit_bytes=mib * 1024 * 1024)


def spot():
    here = lax.axis_index("dp")
    return here // 8, (here // 2) % SIDE, here % 2


def gram_start():
    y, z, _ = spot()
    chip = y * SIDE + z
    shift = (chip % 2) * 64
    return chip * GRAM_ROWS - shift, shift


def pinned(values):
    return [pltpu.with_memory_space_constraint(v, pltpu.VMEM) for v in values]


def device(y, z, core):
    return ((y % SIDE) * SIDE + z % SIDE) * 2 + core


def steps(first, second):
    return [
        (device(y, z, core), device(y + move[0], z + move[1], core))
        for y in range(SIDE)
        for z in range(SIDE)
        for core, move in enumerate((first, second))
    ]


def major(value, step):
    return lax.ppermute(value, "dp", steps((step, 0), (0, step)))


def minor(value, step):
    return lax.ppermute(value, "dp", steps((0, step), (step, 0)))


def along_y(value, step):
    return lax.ppermute(value, "dp", steps((step, 0), (step, 0)))


def along_z(value, step):
    return lax.ppermute(value, "dp", steps((0, step), (0, step)))


def sibling(value):
    return lax.ppermute(value, "dp", [(i, i ^ 1) for i in range(2 * CHIPS)])


def ring(value, move):
    half = value.shape[0] // 2
    up = move(value, 1)
    down = move(value, -1)
    return (up, down, move(up[:half], 1), move(down[half:], -1))


def dispatch_kernel(routes, slots, tokens, *outs):
    wanted = jnp.where(routes[...] < 4, routes[...] * CAP + slots[...], -1)
    lane = lax.broadcasted_iota(jnp.int32, (4 * CAP, 1), 0)
    target = ((lane // CAP + lax.axis_index("expert")) % 4) * CAP + lane % CAP
    hit = wanted[0:1, :] == target
    for k in range(1, 8):
        hit = hit | (wanted[k : k + 1, :] == target)
    one_hot = hit.astype(F32).astype(BF16)
    flag = jnp.max(hit.astype(F32), axis=1, keepdims=True)
    flag = jnp.broadcast_to(flag, (4 * CAP, FLAG)).astype(BF16)
    for start in range(0, WIDTH, 1024):
        rows = jnp.dot(
            one_hot, tokens[:, start : start + 1024], preferred_element_type=F32
        ).astype(BF16)
        for j, out in enumerate(outs):
            out[:, start : start + 1024] = rows[j * CAP : (j + 1) * CAP]
    for j, out in enumerate(outs):
        out[:, WIDTH:] = flag[j * CAP : (j + 1) * CAP]


def dispatch(routes, slots, tokens):
    in_hbm = [pltpu.with_memory_space_constraint(v.T, pltpu.HBM) for v in (routes, slots)]
    return pl.pallas_call(
        dispatch_kernel,
        out_shape=[jax.ShapeDtypeStruct((CAP, SENT), BF16)] * 4,
        in_specs=[VMEM] * 3,
        out_specs=[VMEM] * 4,
        compiler_params=params(32),
    )(*in_hbm, *pinned([tokens]))


def hidden_kernel(spots, first, *refs):
    size = len(refs) - (7 if first else 8)
    height = 64 * len(spots)
    pieces, (g, gs, u, us) = refs[:size], refs[size : size + 4]
    hidden, window, count = refs[-3:]
    y, z, core = spot()
    base, _ = gram_start()
    total = jnp.zeros((height, 256), F32)
    for start in range(0, WIDTH, CHUNK):
        rows = jnp.concatenate([p[:, start : start + CHUNK] for p in pieces], 0)
        weights = jnp.concatenate([w[:, start : start + CHUNK] for w in (g, gs, u, us)], 0)
        total += lax.dot_general(
            rows, weights, (((1,), (1,)), ((), ())), preferred_element_type=F32
        )
    gate, upward = total[:, :128], total[:, 128:]
    value = gate / (1.0 + jnp.exp(-gate)) * upward
    value = jnp.where(core == 1, pltpu.roll(value, 64, 1), value).astype(BF16)
    seen = jnp.concatenate([p[:, WIDTH:] for p in pieces], 0).astype(F32)
    count[...] = jnp.broadcast_to(jnp.sum(seen, axis=0, keepdims=True), (16, FLAG))
    if not first:
        hidden[...] = refs[size + 4][...]
    for j, (far, near) in enumerate(spots):
        far = (jnp.where(core == 0, y, z) + far + SIDE) % SIDE
        near = (jnp.where(core == 0, z, y) + near + SIDE) % SIDE
        slot = jnp.where(core == 0, far * SIDE + near, near * SIDE + far)
        hidden[pl.ds(pl.multiple_of(slot * 64, 64), 64), :] = value[64 * j : 64 * j + 64]
    base = pl.multiple_of(base, 128)
    window[...] = jnp.concatenate([p[:, pl.ds(base, WINDOW)] for p in pieces], 0).T


def hidden_work(spots, pieces, weights, before):
    height = 64 * len(spots)
    return pl.pallas_call(
        functools.partial(hidden_kernel, spots, not before),
        out_shape=[
            jax.ShapeDtypeStruct((1024, 128), BF16),
            jax.ShapeDtypeStruct((WINDOW, height), BF16),
            jax.ShapeDtypeStruct((16, FLAG), F32),
        ],
        in_specs=[VMEM] * (len(pieces) + 4 + len(before)),
        out_specs=[VMEM] * 3,
        compiler_params=params(12),
        cost_estimate=pl.CostEstimate(
            flops=2 * height * 256 * WIDTH,
            bytes_accessed=8 << 20,
            transcendentals=height * 128,
        ),
    )(*pinned(pieces), *pinned(weights), *pinned(before))


def down_kernel(own, z0, z1, z2, y0, y1, y2, *refs):
    counts, (keep, send, tile) = refs[:-3], refs[-3:]
    core = spot()[2]
    left = jnp.concatenate([own[...], z0[...], z1[...], z2[...]], 1)
    right = jnp.concatenate([own[...], y0[...], y1[...], y2[...]], 1)
    tile[...] = lax.dot_general(
        left, right, (((0,), (0,)), ((), ())), preferred_element_type=F32
    )
    for j in range(4):
        mine = pl.multiple_of(128 * j + 64 * core, 64)
        other = pl.multiple_of(128 * j + 64 - 64 * core, 64)
        keep[64 * j : 64 * j + 64, :] = tile[pl.ds(mine, 64), :]
        send[64 * j : 64 * j + 64, :] = tile[pl.ds(other, 64), :].astype(BF16)
    total = sum(n[...] for n in counts)
    high = jnp.floor(total * (1.0 / 32.0)) * 32.0
    zero = jnp.zeros_like(total)
    counts = jnp.concatenate([high, total - high, zero, zero], 1)
    keep[256:, :] = counts
    send[256:, :] = counts.astype(BF16)


def down_work(own, ring_z, ring_y, counts):
    return pl.pallas_call(
        down_kernel,
        out_shape=[
            jax.ShapeDtypeStruct((272, 512), F32),
            jax.ShapeDtypeStruct((272, 512), BF16),
        ],
        in_specs=[VMEM] * (7 + len(counts)),
        out_specs=[VMEM] * 2,
        scratch_shapes=[pltpu.VMEM((512, 512), F32)],
        compiler_params=params(12),
        cost_estimate=pl.CostEstimate(
            flops=2 * 512 * 512 * 1024, bytes_accessed=4 << 20, transcendentals=0
        ),
    )(*pinned((own, *ring_z, *ring_y, *counts)))


def sum_kernel(keep, got, *outs):
    for j in range(4):
        rows = pl.ds(64 * j, 64)
        outs[j][...] = keep[rows, :] + got[rows, :].astype(F32)
    counts = keep[256:264, :] + got[256:, :].astype(F32)[:8]
    total = sum(counts[:, 128 * i : 128 * i + 128] for i in range(4))
    outs[4][...] = 2.0 / total


def sum_blocks(keep, got):
    return pl.pallas_call(
        sum_kernel,
        out_shape=[jax.ShapeDtypeStruct((64, 512), F32)] * 4
        + [jax.ShapeDtypeStruct((8, 128), F32)],
        in_specs=[VMEM] * 2,
        out_specs=[VMEM] * 5,
        compiler_params=params(8),
    )(*pinned((keep, got)))


def place_kernel(b0, b1, b2, b3, factor, out):
    y, z, _ = spot()
    for j, block in enumerate((b0, b1, b2, b3)):
        for i in range(4):
            from_y = (y + ORIGIN[i] + SIDE) % SIDE
            from_z = (z + ORIGIN[j] + SIDE) % SIDE
            start = pl.multiple_of((from_y * SIDE + from_z) * 128, 128)
            part = block[:, 128 * i : 128 * i + 128]
            out[0, :, pl.ds(start, 128)] = part * factor[0:1, :]


def place(blocks, factor):
    return pl.pallas_call(
        place_kernel,
        out_shape=jax.ShapeDtypeStruct((1, 64, FF), F32),
        in_specs=[VMEM] * 5,
        out_specs=VMEM,
        compiler_params=params(8),
    )(*pinned((*blocks, factor)))


def gram_part(windows, pieces, first):
    first = pl.multiple_of(first, 32)
    left = jnp.concatenate([w[pl.ds(first, 224), :] for w in windows], 1)
    here = pl.ds(pl.multiple_of(pl.program_id(0) * CHUNK, CHUNK), CHUNK)
    right = jnp.concatenate([p[:, here] for p in pieces], 0)
    return jnp.dot(left, right, preferred_element_type=F32), here


def gram_rows():
    core = spot()[2]
    _, shift = gram_start()
    return shift + core * 224, shift + 224 - core * 224


def gram_first_kernel(groups, *refs):
    windows, pieces, (keep, send) = refs[:groups], refs[groups:-2], refs[-2:]
    mine, other = gram_rows()
    keep[...], _ = gram_part(windows, pieces, mine)
    send[...], _ = gram_part(windows, pieces, other)


def gram_send_kernel(groups, *refs):
    windows, pieces, (held, send) = refs[:groups], refs[groups:-2], refs[-2:]
    part, here = gram_part(windows, pieces, gram_rows()[1])
    send[...] = (part + held[:, here]).astype(BF16)


def gram_keep_kernel(groups, *refs):
    windows, pieces, (held, got, factor, out) = refs[:groups], refs[groups:-4], refs[-4:]
    part, here = gram_part(windows, pieces, gram_rows()[0])
    out[0, :, :] = (part + held[:, here] + got[:, here].astype(F32)) * factor[0:1, 0:1]


def gram_work(kernel, windows, pieces, others, outs):
    operands = (*windows, *pieces, *others)
    specs = [
        pl.BlockSpec((224, CHUNK), lambda n: (0, n))
        if len(out.shape) == 2
        else pl.BlockSpec((1, 224, CHUNK), lambda n: (0, 0, n))
        for out in outs
    ]
    depth = sum(p.shape[0] for p in pieces)
    return pl.pallas_call(
        functools.partial(kernel, len(windows)),
        grid=(WIDTH // CHUNK,),
        out_shape=outs,
        in_specs=[VMEM] * len(operands),
        out_specs=specs,
        compiler_params=params(10),
        cost_estimate=pl.CostEstimate(
            flops=2 * 224 * WIDTH * depth, bytes_accessed=16 << 20, transcendentals=0
        ),
    )(*pinned(operands))


def after(value, done):
    return lax.optimization_barrier((value, done))


def local(tokens, routes, slot_ids, gate_weight, up_weight):
    gate_own, up_own = gate_weight[0], up_weight[0]
    weights = (gate_own, sibling(gate_own), up_own, sibling(up_own))

    blocks = dispatch(routes, slot_ids, tokens)
    parts = [blocks[0]]
    for step in (1, 2, 3):
        parts.append(lax.ppermute(blocks[step], "expert", [(i, (i + step) % 4) for i in range(4)]))
    shard = jnp.concatenate(parts, 0)
    shard, weights = after(shard, weights)

    up, down, up2, down2 = ring(shard, major)
    far = jnp.concatenate([up2, down2], 0)
    groups = []
    for origin, piece in zip(ORIGIN, (shard, up, down, far)):
        groups.append(((origin,), (piece,) + ring(piece, minor)))
    windows, counts, before = [], [], ()
    first = 0
    for size in (1, 1, 2):
        batch = groups[first : first + size]
        first += size
        spots = [(far, near) for origins, _ in batch for near in ORIGIN for far in origins]
        pieces = [piece for _, group in batch for piece in group]
        hidden, window, count = hidden_work(spots, pieces, weights, before)
        before = (hidden,)
        windows.append(window)
        counts.append(count)
        if len(windows) == 2:
            early = [piece for _, group in groups[:first] for piece in group]
            rows = jax.ShapeDtypeStruct((224, WIDTH), F32)
            keep, send = gram_work(gram_first_kernel, windows, early, (), [rows, rows])
            before, _ = after(before, (keep, send))

    z_down, y_down = along_z(hidden, -1), along_y(hidden, -1)
    y_up, z_far, y_far = along_y(hidden, 1), along_z(hidden, 2), along_y(hidden, 2)
    z_up = along_z(hidden, 1)
    hops = (z_up, z_down, z_far, y_up, y_down, y_far)
    late = [piece for _, group in groups[2:] for piece in group]
    rows = jax.ShapeDtypeStruct((224, WIDTH), BF16)
    (send,) = gram_work(gram_send_kernel, windows[2:], late, (send,), [rows])
    hops, send = after(hops, send)
    down_keep, down_send = down_work(hidden, hops[:3], hops[3:], counts)
    down_got = sibling(down_send)
    send, down_got = after(send, down_got)
    got = sibling(send)
    *sums, factor = sum_blocks(down_keep, down_got)
    down_blocks = [
        sums[0],
        along_z(sums[2], 1),
        along_z(sums[1], -1),
        along_z(sums[3], 2),
    ]
    rows = jax.ShapeDtypeStruct((1, 224, WIDTH), F32)
    (gram,) = gram_work(gram_keep_kernel, windows[2:], late, (keep, got, factor), [rows])
    factor, gram = after(factor, gram)
    return gram, place(down_blocks, factor)


def solution(mesh):
    in_specs = (
        P(("dp", "expert"), None),
        P(("dp", "expert"), None),
        P(("dp", "expert"), None),
        P("expert", "dp", None),
        P("expert", "dp", None),
    )
    out_specs = (P("expert", "dp", None), P("expert", "dp", None))
    return jax.shard_map(local, mesh=mesh, in_specs=in_specs, out_specs=out_specs, check_vma=False)
```

```python
import functools

import jax
import jax.numpy as jnp
from jax import lax
from jax.experimental import pallas as pl
from jax.experimental.pallas import tpu as pltpu
from jax.sharding import PartitionSpec as P

CAP = 16
WIDTH = 7168
FLAG = 128
SENT = WIDTH + FLAG
FF = 2048
SIDE = 4
CHIPS = 16
GRAM_ROWS = 448
WINDOW = 512
F32 = jnp.float32
BF16 = jnp.bfloat16
ORIGIN = (0, -1, 1, 2)
VMEM = pl.BlockSpec(memory_space=pltpu.VMEM)
SMEM = pl.BlockSpec(memory_space=pltpu.SMEM)
CHUNK = 1024


def params(mib):
    return pltpu.CompilerParams(vmem_limit_bytes=mib * 1024 * 1024)


def spot():
    here = lax.axis_index("dp")
    return here // 8, (here // 2) % SIDE, here % 2


def gram_start():
    y, z, _ = spot()
    chip = y * SIDE + z
    shift = (chip % 2) * 64
    return chip * GRAM_ROWS - shift, shift


def pinned(values):
    return [pltpu.with_memory_space_constraint(v, pltpu.VMEM) for v in values]


def device(y, z, core):
    return ((y % SIDE) * SIDE + z % SIDE) * 2 + core


def steps(first, second):
    return [
        (device(y, z, core), device(y + move[0], z + move[1], core))
        for y in range(SIDE)
        for z in range(SIDE)
        for core, move in enumerate((first, second))
    ]


def major(value, step):
    return lax.ppermute(value, "dp", steps((step, 0), (0, step)))


def minor(value, step):
    return lax.ppermute(value, "dp", steps((0, step), (step, 0)))


def along_y(value, step):
    return lax.ppermute(value, "dp", steps((step, 0), (step, 0)))


def along_z(value, step):
    return lax.ppermute(value, "dp", steps((0, step), (0, step)))


def sibling(value):
    return lax.ppermute(value, "dp", [(i, i ^ 1) for i in range(2 * CHIPS)])


def ring(value, move):
    half = value.shape[0] // 2
    up = move(value, 1)
    down = move(value, -1)
    return (up, down, move(up[:half], 1), move(down[half:], -1))


def one_hot_kernel(routes, slots, out, flag):
    wanted = jnp.where(routes[...] < 4, routes[...] * CAP + slots[...], -1)
    lane = lax.broadcasted_iota(jnp.int32, (4 * CAP, 1), 0)
    target = ((lane // CAP + lax.axis_index("expert")) % 4) * CAP + lane % CAP
    hit = wanted[0:1, :] == target
    for k in range(1, 8):
        hit = hit | (wanted[k : k + 1, :] == target)
    hit = hit.astype(F32)
    out[...] = hit.astype(BF16)
    flag[...] = jnp.broadcast_to(jnp.max(hit, axis=1, keepdims=True), (4 * CAP, FLAG)).astype(BF16)


def dispatch_kernel(one_hot, flag, tokens, *outs):
    for start in range(0, WIDTH, 1024):
        rows = jnp.dot(
            one_hot[...], tokens[:, start : start + 1024], preferred_element_type=F32
        ).astype(BF16)
        for j, out in enumerate(outs):
            out[:, start : start + 1024] = rows[j * CAP : (j + 1) * CAP]
    for j, out in enumerate(outs):
        out[:, WIDTH:] = flag[j * CAP : (j + 1) * CAP, :]


def dispatch(routes, slots, tokens):
    in_hbm = [pltpu.with_memory_space_constraint(v.T, pltpu.HBM) for v in (routes, slots)]
    one_hot, flag = pl.pallas_call(
        one_hot_kernel,
        out_shape=[
            jax.ShapeDtypeStruct((4 * CAP, 256), BF16),
            jax.ShapeDtypeStruct((4 * CAP, FLAG), BF16),
        ],
        in_specs=[VMEM] * 2,
        out_specs=[VMEM] * 2,
        compiler_params=params(4),
    )(*in_hbm)
    return pl.pallas_call(
        dispatch_kernel,
        out_shape=[jax.ShapeDtypeStruct((CAP, SENT), BF16)] * 4,
        in_specs=[VMEM] * 3,
        out_specs=[VMEM] * 4,
        compiler_params=params(32),
    )(*pinned((one_hot, flag, tokens)))


def hidden_kernel(spots, first, *refs):
    size = len(refs) - (7 if first else 8)
    height = 64 * len(spots)
    pieces, (g, gs, u, us) = refs[:size], refs[size : size + 4]
    hidden, window, count = refs[-3:]
    y, z, core = spot()
    base, _ = gram_start()
    total = jnp.zeros((height, 256), F32)
    for start in range(0, WIDTH, CHUNK):
        rows = jnp.concatenate([p[:, start : start + CHUNK] for p in pieces], 0)
        weights = jnp.concatenate([w[:, start : start + CHUNK] for w in (g, gs, u, us)], 0)
        total += lax.dot_general(
            rows, weights, (((1,), (1,)), ((), ())), preferred_element_type=F32
        )
    gate, upward = total[:, :128], total[:, 128:]
    value = gate / (1.0 + jnp.exp(-gate)) * upward
    value = jnp.where(core == 1, pltpu.roll(value, 64, 1), value).astype(BF16)
    seen = jnp.concatenate([p[:, WIDTH:] for p in pieces], 0).astype(F32)
    count[...] = jnp.broadcast_to(jnp.sum(seen, axis=0, keepdims=True), (16, FLAG))
    if not first:
        hidden[...] = refs[size + 4][...]
    for j, (far, near) in enumerate(spots):
        far = (jnp.where(core == 0, y, z) + far + SIDE) % SIDE
        near = (jnp.where(core == 0, z, y) + near + SIDE) % SIDE
        slot = jnp.where(core == 0, far * SIDE + near, near * SIDE + far)
        hidden[pl.ds(pl.multiple_of(slot * 64, 64), 64), :] = value[64 * j : 64 * j + 64]
    base = pl.multiple_of(base, 128)
    window[...] = jnp.concatenate([p[:, pl.ds(base, WINDOW)] for p in pieces], 0).T


def hidden_work(spots, pieces, weights, before):
    height = 64 * len(spots)
    return pl.pallas_call(
        functools.partial(hidden_kernel, spots, not before),
        out_shape=[
            jax.ShapeDtypeStruct((1024, 128), BF16),
            jax.ShapeDtypeStruct((WINDOW, height), BF16),
            jax.ShapeDtypeStruct((16, FLAG), F32),
        ],
        in_specs=[VMEM] * (len(pieces) + 4 + len(before)),
        out_specs=[VMEM] * 3,
        compiler_params=params(12),
        cost_estimate=pl.CostEstimate(
            flops=2 * height * 256 * WIDTH,
            bytes_accessed=8 << 20,
            transcendentals=height * 128,
        ),
    )(*pinned(pieces), *pinned(weights), *pinned(before))


def down_kernel(own, z0, z1, z2, y0, y1, y2, *refs):
    counts, (keep, send, tile) = refs[:-3], refs[-3:]
    core = spot()[2]
    left = jnp.concatenate([own[...], z0[...], z1[...], z2[...]], 1)
    right = jnp.concatenate([own[...], y0[...], y1[...], y2[...]], 1)
    tile[...] = lax.dot_general(
        left, right, (((0,), (0,)), ((), ())), preferred_element_type=F32
    )
    for j in range(4):
        mine = pl.multiple_of(128 * j + 64 * core, 64)
        other = pl.multiple_of(128 * j + 64 - 64 * core, 64)
        keep[64 * j : 64 * j + 64, :] = tile[pl.ds(mine, 64), :]
        send[64 * j : 64 * j + 64, :] = tile[pl.ds(other, 64), :].astype(BF16)
    total = sum(n[...] for n in counts)
    high = jnp.floor(total * (1.0 / 32.0)) * 32.0
    zero = jnp.zeros_like(total)
    counts = jnp.concatenate([high, total - high, zero, zero], 1)
    keep[256:, :] = counts
    send[256:, :] = counts.astype(BF16)


def down_work(own, ring_z, ring_y, counts):
    return pl.pallas_call(
        down_kernel,
        out_shape=[
            jax.ShapeDtypeStruct((272, 512), F32),
            jax.ShapeDtypeStruct((272, 512), BF16),
        ],
        in_specs=[VMEM] * (7 + len(counts)),
        out_specs=[VMEM] * 2,
        scratch_shapes=[pltpu.VMEM((512, 512), F32)],
        compiler_params=params(12),
        cost_estimate=pl.CostEstimate(
            flops=2 * 512 * 512 * 1024, bytes_accessed=4 << 20, transcendentals=0
        ),
    )(*pinned((own, *ring_z, *ring_y, *counts)))


def sum_kernel(keep, got, *outs):
    for j in range(4):
        rows = pl.ds(64 * j, 64)
        outs[j][...] = keep[rows, :] + got[rows, :].astype(F32)
    counts = keep[256:264, :] + got[256:, :].astype(F32)[:8]
    total = sum(counts[:, 128 * i : 128 * i + 128] for i in range(4))
    outs[4][...] = 2.0 / total


def sum_blocks(keep, got):
    return pl.pallas_call(
        sum_kernel,
        out_shape=[jax.ShapeDtypeStruct((64, 512), F32)] * 4
        + [jax.ShapeDtypeStruct((8, 128), F32)],
        in_specs=[VMEM] * 2,
        out_specs=[VMEM] * 5,
        compiler_params=params(8),
    )(*pinned((keep, got)))


def place_kernel(b0, b1, b2, b3, factor, out):
    y, z, _ = spot()
    for j, block in enumerate((b0, b1, b2, b3)):
        for i in range(4):
            from_y = (y + ORIGIN[i] + SIDE) % SIDE
            from_z = (z + ORIGIN[j] + SIDE) % SIDE
            start = pl.multiple_of((from_y * SIDE + from_z) * 128, 128)
            part = block[:, 128 * i : 128 * i + 128]
            out[0, :, pl.ds(start, 128)] = part * factor[0:1, :]


def place(blocks, factor):
    return pl.pallas_call(
        place_kernel,
        out_shape=jax.ShapeDtypeStruct((1, 64, FF), F32),
        in_specs=[VMEM] * 5,
        out_specs=VMEM,
        compiler_params=params(8),
    )(*pinned((*blocks, factor)))


def gram_part(windows, pieces, first):
    first = pl.multiple_of(first, 32)
    left = jnp.concatenate([w[pl.ds(first, 224), :] for w in windows], 1)
    here = pl.ds(pl.multiple_of(pl.program_id(0) * CHUNK, CHUNK), CHUNK)
    right = jnp.concatenate([p[:, here] for p in pieces], 0)
    return jnp.dot(left, right, preferred_element_type=F32), here


def gram_rows():
    core = spot()[2]
    _, shift = gram_start()
    return shift + core * 224, shift + 224 - core * 224


def gram_first_kernel(groups, *refs):
    windows, pieces, (keep, send) = refs[:groups], refs[groups:-2], refs[-2:]
    mine, other = gram_rows()
    keep[...], _ = gram_part(windows, pieces, mine)
    send[...], _ = gram_part(windows, pieces, other)


def gram_send_kernel(groups, *refs):
    windows, pieces, (held, send) = refs[:groups], refs[groups:-2], refs[-2:]
    part, here = gram_part(windows, pieces, gram_rows()[1])
    send[...] = (part + held[:, here]).astype(BF16)


def gram_keep_kernel(groups, *refs):
    windows, pieces, (held, got, factor, out) = refs[:groups], refs[groups:-4], refs[-4:]
    part, here = gram_part(windows, pieces, gram_rows()[0])
    out[0, :, :] = (part + held[:, here] + got[:, here].astype(F32)) * factor[0:1, 0:1]


def gram_work(kernel, windows, pieces, others, outs):
    operands = (*windows, *pieces, *others)
    specs = [
        pl.BlockSpec((224, CHUNK), lambda n: (0, n))
        if len(out.shape) == 2
        else pl.BlockSpec((1, 224, CHUNK), lambda n: (0, 0, n))
        for out in outs
    ]
    depth = sum(p.shape[0] for p in pieces)
    return pl.pallas_call(
        functools.partial(kernel, len(windows)),
        grid=(WIDTH // CHUNK,),
        out_shape=outs,
        in_specs=[VMEM] * len(operands),
        out_specs=specs,
        compiler_params=params(10),
        cost_estimate=pl.CostEstimate(
            flops=2 * 224 * WIDTH * depth, bytes_accessed=16 << 20, transcendentals=0
        ),
    )(*pinned(operands))


def after(value, done):
    return lax.optimization_barrier((value, done))


def local(tokens, routes, slot_ids, gate_weight, up_weight):
    gate_own, up_own = gate_weight[0], up_weight[0]
    weights = (gate_own, sibling(gate_own), up_own, sibling(up_own))

    blocks = dispatch(routes, slot_ids, tokens)
    parts = [blocks[0]]
    for step in (1, 2, 3):
        parts.append(lax.ppermute(blocks[step], "expert", [(i, (i + step) % 4) for i in range(4)]))
    shard = jnp.concatenate(parts, 0)
    shard, weights = after(shard, weights)

    up, down, up2, down2 = ring(shard, major)
    far = jnp.concatenate([up2, down2], 0)
    groups = []
    for origin, piece in zip(ORIGIN, (shard, up, down, far)):
        groups.append(((origin,), (piece,) + ring(piece, minor)))
    windows, counts, before = [], [], ()
    first = 0
    for size in (1, 1, 2):
        batch = groups[first : first + size]
        first += size
        spots = [(far, near) for origins, _ in batch for near in ORIGIN for far in origins]
        pieces = [piece for _, group in batch for piece in group]
        hidden, window, count = hidden_work(spots, pieces, weights, before)
        before = (hidden,)
        windows.append(window)
        counts.append(count)
        if len(windows) == 2:
            early = [piece for _, group in groups[:first] for piece in group]
            rows = jax.ShapeDtypeStruct((224, WIDTH), F32)
            keep, send = gram_work(gram_first_kernel, windows, early, (), [rows, rows])
            before, _ = after(before, (keep, send))

    z_down, y_down = along_z(hidden, -1), along_y(hidden, -1)
    y_up, z_far, y_far = along_y(hidden, 1), along_z(hidden, 2), along_y(hidden, 2)
    z_up = along_z(hidden, 1)
    hops = (z_up, z_down, z_far, y_up, y_down, y_far)
    late = [piece for _, group in groups[2:] for piece in group]
    rows = jax.ShapeDtypeStruct((224, WIDTH), BF16)
    (send,) = gram_work(gram_send_kernel, windows[2:], late, (send,), [rows])
    hops, send = after(hops, send)
    down_keep, down_send = down_work(hidden, hops[:3], hops[3:], counts)
    down_got = sibling(down_send)
    send, down_got = after(send, down_got)
    got = sibling(send)
    *sums, factor = sum_blocks(down_keep, down_got)
    down_blocks = [
        sums[0],
        along_z(sums[2], 1),
        along_z(sums[1], -1),
        along_z(sums[3], 2),
    ]
    rows = jax.ShapeDtypeStruct((1, 224, WIDTH), F32)
    (gram,) = gram_work(gram_keep_kernel, windows[2:], late, (keep, got, factor), [rows])
    factor, gram = after(factor, gram)
    return gram, place(down_blocks, factor)


def solution(mesh):
    in_specs = (
        P(("dp", "expert"), None),
        P(("dp", "expert"), None),
        P(("dp", "expert"), None),
        P("expert", "dp", None),
        P("expert", "dp", None),
    )
    out_specs = (P("expert", "dp", None), P("expert", "dp", None))
    return jax.shard_map(local, mesh=mesh, in_specs=in_specs, out_specs=out_specs, check_vma=False)
```
